32 devices in a mesh: groups: 2 (over x), dom: 16 (over z, y, core).
Axes of the slice: x: 2, y: 2, z: 4, core: 2. Of those that a mesh axis runs over, the one named last changes fastest.
Arguments:
- fine_latent: bfloat16 [32768, 256], P(('groups', 'dom')), parts along dimension 0, may hold values from -6 to 6
- pool_owner: int32 [32768, 1], P(('groups', 'dom')), parts along dimension 0, may hold values from 0 to 15, as said below
- pool_local: int32 [32768], P(('groups', 'dom')), parts along dimension 0, may hold values from 0 to 63
- edge_latent: bfloat16 [8192, 256], P(('groups', 'dom')), parts along dimension 0, may hold values from -6 to 6
- src_owner: int32 [8192, 1], P(('groups', 'dom')), parts along dimension 0, may hold values from 0 to 15, as said below
- src_local: int32 [8192], P(('groups', 'dom')), parts along dimension 0, may hold values from 0 to 63
- dst_local: int32 [8192], P(('groups', 'dom')), parts along dimension 0, may hold values from 0 to 63
- edge_w1: bfloat16 [2, 768, 256], replicated, may hold values from -0.21875 to 0.21875
- edge_w2: bfloat16 [2, 256, 256], replicated, may hold values from -0.375 to 0.375
- node_w1: bfloat16 [2, 512, 256], replicated, may hold values from -0.25 to 0.25
- node_w2: bfloat16 [2, 256, 256], replicated, may hold values from -0.375 to 0.375
Outputs:
- fine_out: bfloat16 [32768, 256], P(('groups', 'dom')), parts along dimension 0
The draws below stay inside these ranges and needn't reach their ends.
There are 2 independent parts, one for each index of `groups`. The reference program is written for one: setup_inputs(seed, part) draws one part's arguments, and reference() takes and returns one part's arrays. A program takes and returns all parts, laid end to end along the dimension named above; an argument that names none is the same for every part. Nothing has to cross between parts.
Inputs may be any that keep to these rules, and one draw needn't show every extreme that they name: `pool_owner`: each fine node of device d names d or one of the devices d - 2, d - 1, d + 1, d + 16 / 2 along dom (indices wrap around). Among the fine nodes of one device at most 64 name any one other device, and in every draw the nodes of some device name another device exactly 64 times. `src_owner`: each coarse edge of device d names d or one of the devices d - 2, d - 1, d + 1, d + 16 / 2 along dom (indices wrap around). Among the coarse edges of one device at most 16 name any one other device, and in every draw the edges of some device name another device exactly 16 times.
All inputs are finite; a program needn't handle non-finite values.
Results may differ from the reference program's by a relative error of at most 0.0095.
Values may be sent and summed in bfloat16 or wider, within the bound.
A program may use at most 64 MiB of HBM per device.

```python
import jax
import jax.numpy as jnp
from jax import lax

H = 256
FN_DEV = 1024
LAYERS = 2
CN_DEV = 64
CE_DEV = 256
FINE = 16384
COARSE = 1024
CEDGES = 4096
PCAP = 64
CAP = 16
N_DOM = 16


def nearby_owners(key, rows, most):
    counts = jax.random.randint(key, (N_DOM, 4), 0, most + 1).astype(jnp.int32)
    counts = counts.at[0, 2].set(most)
    counts = counts.at[0, 3].set(most)
    bounds = jnp.cumsum(counts, axis=1)
    places = jnp.arange(rows, dtype=jnp.int32)
    segment = jnp.sum((places[None, :, None] >= bounds[:, None, :]).astype(jnp.int32), axis=2)
    offsets = jnp.array([-2, -1, 1, N_DOM // 2, 0], dtype=jnp.int32)
    labels = offsets[segment]
    row_keys = jax.random.split(jax.random.fold_in(key, 7), N_DOM)
    orders = jax.vmap(lambda one_key: jax.random.permutation(one_key, rows))(row_keys)
    labels = jnp.take_along_axis(labels, orders.astype(jnp.int32), axis=1)
    devices = jnp.arange(N_DOM, dtype=jnp.int32)[:, None]
    return ((devices + labels) % N_DOM).reshape(N_DOM * rows, 1).astype(jnp.int32)


def draw_pool_owner(key, part):
    key = jax.random.fold_in(key, 11)
    return nearby_owners(key, FN_DEV, PCAP)


def draw_src_owner(key, part):
    key = jax.random.fold_in(key, 23)
    return nearby_owners(key, CE_DEV, CAP)


def touch_ends(result, stream_key, low, top_value):
    extent = result.shape
    spot = [jax.random.randint(jax.random.fold_in(stream_key, axis), (), 0, extent[axis]) for axis in range(len(extent))]
    result = result.at[tuple(spot)].set(low)
    longest = extent.index(max(extent))
    spot[longest] = (spot[longest] + 1) % extent[longest]
    return result.at[tuple(spot)].set(top_value)


def levels(stream_key, shape, shards, least, high):
    def one(dim, parts):
        draws = jax.random.uniform(jax.random.fold_in(jax.random.fold_in(stream_key, 6), dim), (parts,), jnp.float32, least / len(shards), high / len(shards))
        return jnp.repeat(jnp.exp(draws), shape[dim] // parts).reshape((-1,) + (1,) * (len(shape) - dim - 1))

    factor_of = one(*shards[0])
    for cut in shards[1:]:
        factor_of = factor_of * one(*cut)
    return factor_of


def scatter_about(rng, shape, scale, bound, pieces=(), kind=jnp.bfloat16):
    factor_of = levels(rng, shape, pieces, -0.22, 0.18) if pieces else 1.0
    entries = jax.random.normal(rng, shape, jnp.float32) * scale * factor_of
    return jnp.minimum(jnp.maximum(entries, -bound), bound).astype(kind)


def setup_inputs(seed: int = 0, part: int = 0) -> dict:
    key_of = jax.random.split(jax.random.key(seed), 12)
    own_keys = jax.random.split(jax.random.fold_in(key_of[11], part), 12)
    return {
        "fine_latent": scatter_about(own_keys[0], (FINE, H), 1.0, 6.0, ((0, 16),)),
        "pool_owner": draw_pool_owner(jax.random.fold_in(jax.random.fold_in(key_of[11], part), 71), part),
        "pool_local": touch_ends(jax.random.randint(own_keys[2], (FINE,), 0, CN_DEV), jax.random.fold_in(own_keys[2], 1), 0, CN_DEV - 1).astype(jnp.int32),
        "edge_latent": scatter_about(own_keys[3], (CEDGES, H), 1.0, 6.0, ((0, 16),)),
        "src_owner": draw_src_owner(jax.random.fold_in(jax.random.fold_in(key_of[11], part), 71), part),
        "src_local": touch_ends(jax.random.randint(own_keys[5], (CEDGES,), 0, CN_DEV), jax.random.fold_in(own_keys[5], 1), 0, CN_DEV - 1).astype(jnp.int32),
        "dst_local": touch_ends(jax.random.randint(own_keys[6], (CEDGES,), 0, CN_DEV), jax.random.fold_in(own_keys[6], 1), 0, CN_DEV - 1).astype(jnp.int32),
        "edge_w1": scatter_about(key_of[7], (LAYERS, 3 * H, H), (3 * H) ** -0.5, 0.21875),
        "edge_w2": scatter_about(key_of[8], (LAYERS, H, H), H ** -0.5, 0.375),
        "node_w1": scatter_about(key_of[9], (LAYERS, 2 * H, H), (2 * H) ** -0.5, 0.25),
        "node_w2": scatter_about(key_of[10], (LAYERS, H, H), H ** -0.5, 0.375),
    }


def layer_norm(values):
    center = values - lax.optimization_barrier(jnp.mean(values, axis=-1, keepdims=True))
    spread = lax.optimization_barrier(jnp.mean(center * center, axis=-1, keepdims=True))
    return center * jax.lax.rsqrt(spread + 1e-05)

def reference(fine_latent, pool_owner, pool_local, edge_latent, src_owner, src_local, dst_local, edge_w1, edge_w2, node_w1, node_w2):
    coarse_index = (pool_owner[:, 0] * CN_DEV + pool_local).astype(jnp.int32)
    senders = (src_owner[:, 0] * CN_DEV + src_local).astype(jnp.int32)
    holders = (jnp.arange(CEDGES, dtype=jnp.int32) // CE_DEV).astype(jnp.int32)
    receivers = (holders * CN_DEV + dst_local).astype(jnp.int32)
    pooled = jax.ops.segment_sum(fine_latent.astype(jnp.float32), coarse_index, num_segments=COARSE)
    coarse = (pooled * 0.25).astype(jnp.bfloat16)
    edge_state = edge_latent
    for layer_index in range(LAYERS):
        joined = jnp.concatenate([coarse[senders], coarse[receivers], edge_state], axis=1)
        hidden = jax.nn.relu(jnp.dot(joined, edge_w1[layer_index], preferred_element_type=jnp.float32)).astype(jnp.bfloat16)
        update = layer_norm(jnp.dot(hidden, edge_w2[layer_index], preferred_element_type=jnp.float32))
        edge_state = (edge_state.astype(jnp.float32) + update).astype(jnp.bfloat16)
        summed = jax.ops.segment_sum(edge_state.astype(jnp.float32), receivers, num_segments=COARSE).astype(jnp.bfloat16)
        joined = jnp.concatenate([coarse, summed], axis=1)
        hidden = jax.nn.relu(jnp.dot(joined, node_w1[layer_index], preferred_element_type=jnp.float32)).astype(jnp.bfloat16)
        update = layer_norm(jnp.dot(hidden, node_w2[layer_index], preferred_element_type=jnp.float32))
        coarse = (coarse.astype(jnp.float32) + update).astype(jnp.bfloat16)
    lifted = coarse[coarse_index].astype(jnp.float32)
    return (fine_latent.astype(jnp.float32) + lifted).astype(jnp.bfloat16)
```

```python
import functools

import jax
import jax.numpy as jnp
from jax import lax
from jax.experimental import pallas as pl
from jax.experimental.pallas import tpu as pltpu
from jax.sharding import PartitionSpec as P

LAYERS = 2
FINE_PER_COARSE = 16
CAP = 16
PARTNERS = 4
FAR = 3
CHUNKS = 4
ORDER = (3, 0, 1, 2)


def dot(a, b):
    return jnp.dot(a, b, preferred_element_type=jnp.float32)


def layer_norm(values):
    center = values - jnp.mean(values, axis=-1, keepdims=True)
    spread = jnp.mean(center * center, axis=-1, keepdims=True)
    return center * lax.rsqrt(spread + 1e-05)


def iota(shape, dim):
    return lax.broadcasted_iota(jnp.int32, shape, dim).astype(jnp.float32)


def onehot(a, b):
    return jnp.where(a == b, 1.0, 0.0).astype(jnp.bfloat16)


def to_column(row):
    wide = jnp.broadcast_to(row, (8, row.shape[1]))
    return jnp.transpose(wide)[:, 0:1]


def kernel(
    n,
    fine_hbm,
    pool_owner,
    pool_local,
    edge_hbm,
    src_owner,
    src_local,
    dst_local,
    ew1_hbm,
    ew2_hbm,
    nw1_hbm,
    nw2_hbm,
    out_hbm,
    fine,
    edges,
    ew1,
    ew2,
    nw1,
    nw2,
    lift_base,
    out,
    pool_send,
    pool_recv,
    want_send,
    want_recv,
    rows_send,
    rows_recv,
    last_send,
    last_recv,
    load_sem,
    store_sem,
    send_sem,
    recv_sem,
):
    fine_rows, width = fine.shape
    cn = fine_rows // FINE_PER_COARSE
    edge_rows = edges.shape[0]
    me = lax.axis_index("dom")
    offsets = (n - 2, n - 1, 1, n // 2)

    def ahead(k):
        return lax.rem(me + offsets[k], n)

    def behind(k):
        return lax.rem(me + n - offsets[k], n)

    barrier = pltpu.get_barrier_semaphore()
    for step in (1, 2, n // 2, n - 2, n - 1):
        pl.semaphore_signal(
            barrier,
            inc=1,
            device_id={"dom": lax.rem(me + step, n)},
            device_id_type=pl.DeviceIdType.MESH,
        )

    step_rows = fine_rows // CHUNKS
    loads = []
    for c in range(CHUNKS):
        part = pl.ds(c * step_rows, step_rows)
        loads.append((fine_hbm.at[part], fine.at[part]))
    loads += [
        (edge_hbm, edges),
        (ew1_hbm, ew1),
        (ew2_hbm, ew2),
        (nw1_hbm, nw1),
        (nw2_hbm, nw2),
    ]
    loads = [
        pltpu.make_async_copy(src, dst, load_sem.at[i]) for i, (src, dst) in enumerate(loads)
    ]
    for copy in loads:
        copy.start()

    def remote(stage, k, src, dst, target):
        return pltpu.make_async_remote_copy(
            src_ref=src,
            dst_ref=dst,
            send_sem=send_sem.at[stage, k],
            recv_sem=recv_sem.at[stage, k],
            device_id={"dom": target},
            device_id_type=pl.DeviceIdType.MESH,
        )

    def slot(owner):
        rel = owner - me
        rel = jnp.where(rel < 0, rel + n, rel)
        k = jnp.where(rel == 0, PARTNERS, FAR)
        for j in range(FAR):
            k = jnp.where(rel == offsets[j], j, k)
        return k

    pool_row = (slot(pool_owner[...]) * cn + pool_local[...]).astype(jnp.float32)
    total = jnp.zeros((PARTNERS * cn, width), jnp.float32)
    own = jnp.zeros((cn, width), jnp.float32)
    for c in range(CHUNKS):
        piece = pool_row[:, c * step_rows : (c + 1) * step_rows]
        away = onehot(piece, iota((PARTNERS * cn, step_rows), 0))
        loads[c].wait()
        total += dot(away, fine[pl.ds(c * step_rows, step_rows), :])
    pool_send[...] = total.astype(jnp.bfloat16)
    pl.semaphore_wait(barrier, 5)
    sends = []
    pool_copies = [
        remote(0, k, pool_send.at[pl.ds(k * cn, cn)], pool_recv.at[pl.ds(k * cn, cn)], ahead(k))
        for k in range(PARTNERS)
    ]
    for k in ORDER:
        pool_copies[k].start()
    sends += pool_copies

    src_slot = slot(src_owner[...])
    src_row = src_local[...].astype(jnp.float32)
    dst_row = dst_local[...].astype(jnp.float32)
    slot_row = src_slot.astype(jnp.float32)
    by_slot = onehot(slot_row, iota((8, edge_rows), 0))
    earlier = jnp.where(
        iota((edge_rows, edge_rows), 0) < iota((edge_rows, edge_rows), 1), 1.0, 0.0
    ).astype(jnp.bfloat16)
    ranks = dot(by_slot, earlier)
    rank = jnp.sum(ranks * by_slot.astype(jnp.float32), axis=0, keepdims=True)
    away_row = jnp.where(src_slot < PARTNERS, slot_row * CAP + rank, -1.0)
    own_src_row = jnp.where(src_slot < PARTNERS, -1.0, src_row)
    src_col = to_column(src_row)
    want = dot(
        onehot(away_row, iota((PARTNERS * CAP, edge_rows), 0)),
        onehot(src_col, iota((edge_rows, want_send.shape[1]), 1)),
    )
    want_send[...] = want.astype(jnp.bfloat16)
    want_copies = [
        remote(
            1, k, want_send.at[pl.ds(k * CAP, CAP)], want_recv.at[pl.ds(k * CAP, CAP)], ahead(k)
        )
        for k in range(PARTNERS)
    ]
    for k in ORDER:
        want_copies[k].start()
    sends += want_copies

    for c in range(CHUNKS):
        piece = pool_row[:, c * step_rows : (c + 1) * step_rows] - PARTNERS * cn
        own += dot(
            onehot(piece, iota((cn, step_rows), 0)), fine[pl.ds(c * step_rows, step_rows), :]
        )
    take_away = onehot(to_column(away_row), iota((edge_rows, PARTNERS * CAP), 1))
    take_own = onehot(to_column(own_src_row), iota((edge_rows, cn), 1))
    take_dst = onehot(to_column(dst_row), iota((edge_rows, cn), 1))
    add_dst = onehot(dst_row, iota((cn, edge_rows), 0))
    pool_col = to_column(pool_row)
    for copy in loads[CHUNKS:]:
        copy.wait()
    edge_state = edges[...]

    for copy in pool_copies:
        copy.wait_recv()
    for k in range(PARTNERS):
        own += pool_recv[pl.ds(k * cn, cn), :].astype(jnp.float32)
    coarse = (own * 0.25).astype(jnp.bfloat16)
    for copy in want_copies:
        copy.wait_recv()

    for layer in range(LAYERS):
        rows_send[layer] = dot(want_recv[:, :cn], coarse).astype(jnp.bfloat16)
        row_copies = [
            remote(
                2 + layer,
                k,
                rows_send.at[layer, pl.ds(k * CAP, CAP)],
                rows_recv.at[layer, pl.ds(k * CAP, CAP)],
                behind(k),
            )
            for k in range(PARTNERS)
        ]
        for k in ORDER:
            row_copies[k].start()
        sends += row_copies
        mixed = dot(edge_state, ew1[layer, 2 * width :, :])
        mixed += dot(dot(take_own, coarse).astype(jnp.bfloat16), ew1[layer, :width, :])
        mixed += dot(dot(take_dst, coarse).astype(jnp.bfloat16), ew1[layer, width : 2 * width, :])
        node_mixed = dot(coarse, nw1[layer, :width, :])
        for copy in row_copies:
            copy.wait_recv()
        sender = dot(take_away, rows_recv[layer]).astype(jnp.bfloat16)
        mixed += dot(sender, ew1[layer, :width, :])
        hidden = jnp.maximum(mixed, 0.0).astype(jnp.bfloat16)
        update = layer_norm(dot(hidden, ew2[layer]))
        edge_state = (edge_state.astype(jnp.float32) + update).astype(jnp.bfloat16)
        summed = dot(add_dst, edge_state).astype(jnp.bfloat16)
        node_mixed += dot(summed, nw1[layer, width:, :])
        hidden = jnp.maximum(node_mixed, 0.0).astype(jnp.bfloat16)
        update = layer_norm(dot(hidden, nw2[layer]))
        coarse = (coarse.astype(jnp.float32) + update).astype(jnp.bfloat16)

    last_send[...] = coarse
    last_copies = [
        remote(2 + LAYERS, k, last_send, last_recv.at[pl.ds(k * cn, cn)], behind(k))
        for k in range(PARTNERS)
    ]
    for k in ORDER:
        last_copies[k].start()
    sends += last_copies
    take_base = onehot(pool_col - PARTNERS * cn, iota((fine_rows, cn), 1))
    lift_base[...] = fine[...].astype(jnp.float32) + dot(take_base, coarse)
    take_far = onehot(pool_col, iota((fine_rows, PARTNERS * cn), 1))
    for copy in last_copies:
        copy.wait_recv()
    stores = []
    for c in range(CHUNKS):
        part = pl.ds(c * step_rows, step_rows)
        lifted = dot(take_far[c * step_rows : (c + 1) * step_rows], last_recv[...])
        out[part, :] = (lift_base[part, :] + lifted).astype(jnp.bfloat16)
        copy = pltpu.make_async_copy(out.at[part], out_hbm.at[part], store_sem.at[c])
        copy.start()
        stores.append(copy)
    for copy in sends:
        copy.wait_send()
    for copy in stores:
        copy.wait()


def per_device(
    n,
    fine_latent,
    pool_owner,
    pool_local,
    edge_latent,
    src_owner,
    src_local,
    dst_local,
    edge_w1,
    edge_w2,
    node_w1,
    node_w2,
):
    fine_rows, width = fine_latent.shape
    edge_rows = edge_latent.shape[0]
    cn = fine_rows // FINE_PER_COARSE
    lanes = -(-cn // 128) * 128
    hbm = pl.BlockSpec(memory_space=pl.ANY)
    vmem = pl.BlockSpec(memory_space=pltpu.VMEM)
    bf16 = jnp.bfloat16
    stages = 3 + LAYERS
    return pl.pallas_call(
        functools.partial(kernel, n),
        out_shape=jax.ShapeDtypeStruct((fine_rows, width), bf16),
        in_specs=[hbm, vmem, vmem, hbm, vmem, vmem, vmem, hbm, hbm, hbm, hbm],
        out_specs=hbm,
        scratch_shapes=[
            pltpu.VMEM((fine_rows, width), bf16),
            pltpu.VMEM((edge_rows, width), bf16),
            pltpu.VMEM(edge_w1.shape, bf16),
            pltpu.VMEM(edge_w2.shape, bf16),
            pltpu.VMEM(node_w1.shape, bf16),
            pltpu.VMEM(node_w2.shape, bf16),
            pltpu.VMEM((fine_rows, width), jnp.float32),
            pltpu.VMEM((fine_rows, width), bf16),
            pltpu.VMEM((PARTNERS * cn, width), bf16),
            pltpu.VMEM((PARTNERS * cn, width), bf16),
            pltpu.VMEM((PARTNERS * CAP, lanes), bf16),
            pltpu.VMEM((PARTNERS * CAP, lanes), bf16),
            pltpu.VMEM((LAYERS, PARTNERS * CAP, width), bf16),
            pltpu.VMEM((LAYERS, PARTNERS * CAP, width), bf16),
            pltpu.VMEM((cn, width), bf16),
            pltpu.VMEM((PARTNERS * cn, width), bf16),
            pltpu.SemaphoreType.DMA((CHUNKS + 5,)),
            pltpu.SemaphoreType.DMA((CHUNKS,)),
            pltpu.SemaphoreType.DMA((stages, PARTNERS)),
            pltpu.SemaphoreType.DMA((stages, PARTNERS)),
        ],
        compiler_params=pltpu.CompilerParams(
            collective_id=0, has_side_effects=True, vmem_limit_bytes=60 * 1024 * 1024
        ),
    )(
        fine_latent,
        pool_owner.reshape(1, fine_rows),
        pool_local.reshape(1, fine_rows),
        edge_latent,
        src_owner.reshape(1, edge_rows),
        src_local.reshape(1, edge_rows),
        dst_local.reshape(1, edge_rows),
        edge_w1,
        edge_w2,
        node_w1,
        node_w2,
    )


def solution(mesh):
    rows = P(("groups", "dom"), None)
    line = P(("groups", "dom"))
    return jax.shard_map(
        functools.partial(per_device, mesh.shape["dom"]),
        mesh=mesh,
        in_specs=(rows, rows, line, rows, rows, line, line, P(), P(), P(), P()),
        out_specs=rows,
        check_vma=False,
    )
```

```python
import functools

import jax
import jax.numpy as jnp
from jax import lax
from jax.experimental import pallas as pl
from jax.experimental.pallas import tpu as pltpu
from jax.sharding import PartitionSpec as P

LAYERS = 2
FINE_PER_COARSE = 16
CAP = 16
PARTNERS = 4
FAR = 3
CHUNKS = 4
ORDER = (1, 2, 0, 3)


def dot(a, b):
    return jnp.dot(a, b, preferred_element_type=jnp.float32)


def layer_norm(values):
    center = values - jnp.mean(values, axis=-1, keepdims=True)
    spread = jnp.mean(center * center, axis=-1, keepdims=True)
    return center * lax.rsqrt(spread + 1e-05)


def iota(shape, dim):
    return lax.broadcasted_iota(jnp.int32, shape, dim).astype(jnp.float32)


def onehot(a, b):
    return jnp.where(a == b, 1.0, 0.0).astype(jnp.bfloat16)


def to_column(row):
    wide = jnp.broadcast_to(row, (8, row.shape[1]))
    return jnp.transpose(wide)[:, 0:1]


def kernel(
    n,
    fine_hbm,
    pool_owner_hbm,
    pool_local_hbm,
    edge_hbm,
    src_owner_hbm,
    src_local_hbm,
    dst_local_hbm,
    ew1_hbm,
    ew2_hbm,
    nw1_hbm,
    nw2_hbm,
    out,
    pool_owner,
    pool_local,
    src_owner,
    src_local,
    dst_local,
    fine,
    edges,
    ew1,
    ew2,
    nw1,
    nw2,
    lift_base,
    pool_send,
    pool_recv,
    want_send,
    want_recv,
    rows_send,
    rows_recv,
    last_send,
    last_recv,
    load_sem,
    send_sem,
    recv_sem,
):
    fine_rows, width = fine.shape
    cn = fine_rows // FINE_PER_COARSE
    edge_rows = edges.shape[0]
    me = lax.axis_index("dom")
    offsets = (n - 2, n - 1, 1, n // 2)

    def ahead(k):
        return lax.rem(me + offsets[k], n)

    def behind(k):
        return lax.rem(me + n - offsets[k], n)

    barrier = pltpu.get_barrier_semaphore()
    for step in (1, n - 1, 2, n - 2, n // 2):
        pl.semaphore_signal(
            barrier,
            inc=1,
            device_id={"dom": lax.rem(me + step, n)},
            device_id_type=pl.DeviceIdType.MESH,
        )

    step_rows = fine_rows // CHUNKS
    loads = [(pool_owner_hbm, pool_owner), (pool_local_hbm, pool_local)]
    for c in range(CHUNKS):
        part = pl.ds(c * step_rows, step_rows)
        loads.append((fine_hbm.at[part], fine.at[part]))
    loads += [
        (src_owner_hbm, src_owner),
        (src_local_hbm, src_local),
        (dst_local_hbm, dst_local),
        (edge_hbm, edges),
        (ew1_hbm, ew1),
        (ew2_hbm, ew2),
        (nw1_hbm, nw1),
        (nw2_hbm, nw2),
    ]
    loads = [
        pltpu.make_async_copy(src, dst, load_sem.at[i]) for i, (src, dst) in enumerate(loads)
    ]
    for copy in loads:
        copy.start()

    def remote(stage, k, src, dst, target):
        return pltpu.make_async_remote_copy(
            src_ref=src,
            dst_ref=dst,
            send_sem=send_sem.at[stage, k],
            recv_sem=recv_sem.at[stage, k],
            device_id={"dom": target},
            device_id_type=pl.DeviceIdType.MESH,
        )

    def slot(owner):
        rel = owner - me
        rel = jnp.where(rel < 0, rel + n, rel)
        k = jnp.where(rel == 0, PARTNERS, FAR)
        for j in range(FAR):
            k = jnp.where(rel == offsets[j], j, k)
        return k

    def arrive(first, last):
        for copy in loads[first:last]:
            copy.wait()

    arrive(0, 2)
    pool_row = (slot(pool_owner[...]) * cn + pool_local[...]).astype(jnp.float32)
    total = jnp.zeros((PARTNERS * cn, width), jnp.float32)
    own = jnp.zeros((cn, width), jnp.float32)
    for c in range(CHUNKS):
        piece = pool_row[:, c * step_rows : (c + 1) * step_rows]
        away = onehot(piece, iota((PARTNERS * cn, step_rows), 0))
        arrive(2 + c, 3 + c)
        total += dot(away, fine[pl.ds(c * step_rows, step_rows), :])
    pool_send[...] = total.astype(jnp.bfloat16)
    pl.semaphore_wait(barrier, 5)
    sends = []
    pool_copies = [
        remote(0, k, pool_send.at[pl.ds(k * cn, cn)], pool_recv.at[pl.ds(k * cn, cn)], ahead(k))
        for k in range(PARTNERS)
    ]
    for k in ORDER:
        pool_copies[k].start()
    sends += pool_copies

    arrive(2 + CHUNKS, 5 + CHUNKS)
    src_slot = slot(src_owner[...])
    src_row = src_local[...].astype(jnp.float32)
    dst_row = dst_local[...].astype(jnp.float32)
    slot_row = src_slot.astype(jnp.float32)
    by_slot = onehot(slot_row, iota((8, edge_rows), 0))
    earlier = jnp.where(
        iota((edge_rows, edge_rows), 0) < iota((edge_rows, edge_rows), 1), 1.0, 0.0
    ).astype(jnp.bfloat16)
    ranks = dot(by_slot, earlier)
    rank = jnp.sum(ranks * by_slot.astype(jnp.float32), axis=0, keepdims=True)
    away_row = jnp.where(src_slot < PARTNERS, slot_row * CAP + rank, -1.0)
    own_src_row = jnp.where(src_slot < PARTNERS, -1.0, src_row)
    src_col = to_column(src_row)
    want = dot(
        onehot(away_row, iota((PARTNERS * CAP, edge_rows), 0)),
        onehot(src_col, iota((edge_rows, want_send.shape[1]), 1)),
    )
    want_send[...] = want.astype(jnp.bfloat16)
    want_copies = [
        remote(
            1, k, want_send.at[pl.ds(k * CAP, CAP)], want_recv.at[pl.ds(k * CAP, CAP)], ahead(k)
        )
        for k in range(PARTNERS)
    ]
    for k in ORDER:
        want_copies[k].start()
    sends += want_copies

    for c in range(CHUNKS):
        piece = pool_row[:, c * step_rows : (c + 1) * step_rows] - PARTNERS * cn
        own += dot(
            onehot(piece, iota((cn, step_rows), 0)), fine[pl.ds(c * step_rows, step_rows), :]
        )
    take_away = onehot(to_column(away_row), iota((edge_rows, PARTNERS * CAP), 1))
    take_own = onehot(to_column(own_src_row), iota((edge_rows, cn), 1))
    take_dst = onehot(to_column(dst_row), iota((edge_rows, cn), 1))
    add_dst = onehot(dst_row, iota((cn, edge_rows), 0))
    pool_col = to_column(pool_row)
    arrive(5 + CHUNKS, len(loads))
    edge_state = edges[...]

    for copy in pool_copies:
        copy.wait_recv()
    for k in range(PARTNERS):
        own += pool_recv[pl.ds(k * cn, cn), :].astype(jnp.float32)
    coarse = (own * 0.25).astype(jnp.bfloat16)
    for copy in want_copies:
        copy.wait_recv()

    for layer in range(LAYERS):
        rows_send[layer] = dot(want_recv[:, :cn], coarse).astype(jnp.bfloat16)
        row_copies = [
            remote(
                2 + layer,
                k,
                rows_send.at[layer, pl.ds(k * CAP, CAP)],
                rows_recv.at[layer, pl.ds(k * CAP, CAP)],
                behind(k),
            )
            for k in range(PARTNERS)
        ]
        for k in ORDER:
            row_copies[k].start()
        sends += row_copies
        mixed = dot(edge_state, ew1[layer, 2 * width :, :])
        mixed += dot(dot(take_own, coarse).astype(jnp.bfloat16), ew1[layer, :width, :])
        mixed += dot(dot(take_dst, coarse).astype(jnp.bfloat16), ew1[layer, width : 2 * width, :])
        node_mixed = dot(coarse, nw1[layer, :width, :])
        for copy in row_copies:
            copy.wait_recv()
        sender = dot(take_away, rows_recv[layer]).astype(jnp.bfloat16)
        mixed += dot(sender, ew1[layer, :width, :])
        hidden = jnp.maximum(mixed, 0.0).astype(jnp.bfloat16)
        update = layer_norm(dot(hidden, ew2[layer]))
        edge_state = (edge_state.astype(jnp.float32) + update).astype(jnp.bfloat16)
        summed = dot(add_dst, edge_state).astype(jnp.bfloat16)
        node_mixed += dot(summed, nw1[layer, width:, :])
        hidden = jnp.maximum(node_mixed, 0.0).astype(jnp.bfloat16)
        update = layer_norm(dot(hidden, nw2[layer]))
        coarse = (coarse.astype(jnp.float32) + update).astype(jnp.bfloat16)

    last_send[...] = coarse
    last_copies = [
        remote(2 + LAYERS, k, last_send, last_recv.at[pl.ds(k * cn, cn)], behind(k))
        for k in range(PARTNERS)
    ]
    for k in ORDER:
        last_copies[k].start()
    sends += last_copies
    take_base = onehot(pool_col - PARTNERS * cn, iota((fine_rows, cn), 1))
    lift_base[...] = fine[...].astype(jnp.float32) + dot(take_base, coarse)
    take_far = onehot(pool_col, iota((fine_rows, PARTNERS * cn), 1))
    for copy in last_copies:
        copy.wait_recv()
    for c in range(CHUNKS):
        part = pl.ds(c * step_rows, step_rows)
        lifted = dot(take_far[c * step_rows : (c + 1) * step_rows], last_recv[...])
        out[part, :] = (lift_base[part, :] + lifted).astype(jnp.bfloat16)
    for copy in sends:
        copy.wait_send()


def per_device(
    n,
    fine_latent,
    pool_owner,
    pool_local,
    edge_latent,
    src_owner,
    src_local,
    dst_local,
    edge_w1,
    edge_w2,
    node_w1,
    node_w2,
):
    fine_rows, width = fine_latent.shape
    edge_rows = edge_latent.shape[0]
    cn = fine_rows // FINE_PER_COARSE
    lanes = -(-cn // 128) * 128
    hbm = pl.BlockSpec(memory_space=pltpu.HBM)
    vmem = pl.BlockSpec(memory_space=pltpu.VMEM)
    bf16 = jnp.bfloat16
    stages = 3 + LAYERS
    return pl.pallas_call(
        functools.partial(kernel, n),
        out_shape=pltpu.VMEM((fine_rows, width), bf16),
        in_specs=[hbm] * 11,
        out_specs=vmem,
        scratch_shapes=[
            pltpu.VMEM((1, fine_rows), jnp.int32),
            pltpu.VMEM((1, fine_rows), jnp.int32),
            pltpu.VMEM((1, edge_rows), jnp.int32),
            pltpu.VMEM((1, edge_rows), jnp.int32),
            pltpu.VMEM((1, edge_rows), jnp.int32),
            pltpu.VMEM((fine_rows, width), bf16),
            pltpu.VMEM((edge_rows, width), bf16),
            pltpu.VMEM(edge_w1.shape, bf16),
            pltpu.VMEM(edge_w2.shape, bf16),
            pltpu.VMEM(node_w1.shape, bf16),
            pltpu.VMEM(node_w2.shape, bf16),
            pltpu.VMEM((fine_rows, width), jnp.float32),
            pltpu.VMEM((PARTNERS * cn, width), bf16),
            pltpu.VMEM((PARTNERS * cn, width), bf16),
            pltpu.VMEM((PARTNERS * CAP, lanes), bf16),
            pltpu.VMEM((PARTNERS * CAP, lanes), bf16),
            pltpu.VMEM((LAYERS, PARTNERS * CAP, width), bf16),
            pltpu.VMEM((LAYERS, PARTNERS * CAP, width), bf16),
            pltpu.VMEM((cn, width), bf16),
            pltpu.VMEM((PARTNERS * cn, width), bf16),
            pltpu.SemaphoreType.DMA((CHUNKS + 10,)),
            pltpu.SemaphoreType.DMA((stages, PARTNERS)),
            pltpu.SemaphoreType.DMA((stages, PARTNERS)),
        ],
        compiler_params=pltpu.CompilerParams(
            collective_id=0, has_side_effects=True, vmem_limit_bytes=60 * 1024 * 1024
        ),
    )(
        fine_latent,
        pool_owner.reshape(1, fine_rows),
        pool_local.reshape(1, fine_rows),
        edge_latent,
        src_owner.reshape(1, edge_rows),
        src_local.reshape(1, edge_rows),
        dst_local.reshape(1, edge_rows),
        edge_w1,
        edge_w2,
        node_w1,
        node_w2,
    )


def solution(mesh):
    rows = P(("groups", "dom"), None)
    line = P(("groups", "dom"))
    return jax.shard_map(
        functools.partial(per_device, mesh.shape["dom"]),
        mesh=mesh,
        in_specs=(rows, rows, line, rows, rows, line, line, P(), P(), P(), P()),
        out_specs=rows,
        check_vma=False,
    )
```

```python
import functools

import jax
import jax.numpy as jnp
from jax import lax
from jax.experimental import pallas as pl
from jax.experimental.pallas import tpu as pltpu
from jax.sharding import PartitionSpec as P

LAYERS = 2
FINE_PER_COARSE = 16
CAP = 16
PARTNERS = 4
FAR = 3
CHUNKS = 4
ORDER = (1, 2, 0, 3)


def dot(a, b):
    return jnp.dot(a, b, preferred_element_type=jnp.float32)


def layer_norm(values):
    center = values - jnp.mean(values, axis=-1, keepdims=True)
    spread = jnp.mean(center * center, axis=-1, keepdims=True)
    return center * lax.rsqrt(spread + 1e-05)


def iota(shape, dim):
    return lax.broadcasted_iota(jnp.int32, shape, dim).astype(jnp.float32)


def onehot(a, b):
    return jnp.where(a == b, 1.0, 0.0).astype(jnp.bfloat16)


def to_column(row):
    wide = jnp.broadcast_to(row, (8, row.shape[1]))
    return jnp.transpose(wide)[:, 0:1]


def kernel(
    n,
    fine_hbm,
    pool_owner_hbm,
    pool_local_hbm,
    edge_hbm,
    src_owner_hbm,
    src_local_hbm,
    dst_local_hbm,
    ew1_hbm,
    ew2_hbm,
    nw1_hbm,
    nw2_hbm,
    lift_base,
    take_far,
    lift_rows,
    pool_owner,
    pool_local,
    src_owner,
    src_local,
    dst_local,
    fine,
    edges,
    ew1,
    ew2,
    nw1,
    nw2,
    pool_send,
    pool_recv,
    want_send,
    want_recv,
    rows_send,
    rows_recv,
    last_send,
    last_recv,
    load_sem,
    send_sem,
    recv_sem,
):
    fine_rows, width = fine.shape
    cn = fine_rows // FINE_PER_COARSE
    edge_rows = edges.shape[0]
    me = lax.axis_index("dom")
    offsets = (n - 2, n - 1, 1, n // 2)

    def ahead(k):
        return lax.rem(me + offsets[k], n)

    def behind(k):
        return lax.rem(me + n - offsets[k], n)

    barrier = pltpu.get_barrier_semaphore()
    for step in (1, n - 1, 2, n - 2, n // 2):
        pl.semaphore_signal(
            barrier,
            inc=1,
            device_id={"dom": lax.rem(me + step, n)},
            device_id_type=pl.DeviceIdType.MESH,
        )

    step_rows = fine_rows // CHUNKS
    loads = [(pool_owner_hbm, pool_owner), (pool_local_hbm, pool_local)]
    for c in range(CHUNKS):
        part = pl.ds(c * step_rows, step_rows)
        loads.append((fine_hbm.at[part], fine.at[part]))
    loads += [
        (src_owner_hbm, src_owner),
        (src_local_hbm, src_local),
        (dst_local_hbm, dst_local),
        (edge_hbm, edges),
        (ew1_hbm, ew1),
        (ew2_hbm, ew2),
        (nw1_hbm, nw1),
        (nw2_hbm, nw2),
    ]
    loads = [
        pltpu.make_async_copy(src, dst, load_sem.at[i]) for i, (src, dst) in enumerate(loads)
    ]
    for copy in loads:
        copy.start()

    def remote(stage, k, src, dst, target):
        return pltpu.make_async_remote_copy(
            src_ref=src,
            dst_ref=dst,
            send_sem=send_sem.at[stage, k],
            recv_sem=recv_sem.at[stage, k],
            device_id={"dom": target},
            device_id_type=pl.DeviceIdType.MESH,
        )

    def slot(owner):
        rel = owner - me
        rel = jnp.where(rel < 0, rel + n, rel)
        k = jnp.where(rel == 0, PARTNERS, FAR)
        for j in range(FAR):
            k = jnp.where(rel == offsets[j], j, k)
        return k

    def arrive(first, last):
        for copy in loads[first:last]:
            copy.wait()

    arrive(0, 2)
    pool_row = (slot(pool_owner[...]) * cn + pool_local[...]).astype(jnp.float32)
    total = jnp.zeros((PARTNERS * cn, width), jnp.float32)
    own = jnp.zeros((cn, width), jnp.float32)
    for c in range(CHUNKS):
        piece = pool_row[:, c * step_rows : (c + 1) * step_rows]
        away = onehot(piece, iota((PARTNERS * cn, step_rows), 0))
        arrive(2 + c, 3 + c)
        total += dot(away, fine[pl.ds(c * step_rows, step_rows), :])
    pool_send[...] = total.astype(jnp.bfloat16)
    pl.semaphore_wait(barrier, 5)
    sends = []
    pool_copies = [
        remote(0, k, pool_send.at[pl.ds(k * cn, cn)], pool_recv.at[pl.ds(k * cn, cn)], ahead(k))
        for k in range(PARTNERS)
    ]
    for k in (1, 0, 2, 3):
        pool_copies[k].start()
    sends += pool_copies

    arrive(2 + CHUNKS, 5 + CHUNKS)
    src_slot = slot(src_owner[...])
    src_row = src_local[...].astype(jnp.float32)
    dst_row = dst_local[...].astype(jnp.float32)
    slot_row = src_slot.astype(jnp.float32)
    by_slot = onehot(slot_row, iota((8, edge_rows), 0))
    earlier = jnp.where(
        iota((edge_rows, edge_rows), 0) < iota((edge_rows, edge_rows), 1), 1.0, 0.0
    ).astype(jnp.bfloat16)
    ranks = dot(by_slot, earlier)
    rank = jnp.sum(ranks * by_slot.astype(jnp.float32), axis=0, keepdims=True)
    away_row = jnp.where(src_slot < PARTNERS, slot_row * CAP + rank, -1.0)
    own_src_row = jnp.where(src_slot < PARTNERS, -1.0, src_row)
    src_col = to_column(src_row)
    want = dot(
        onehot(away_row, iota((PARTNERS * CAP, edge_rows), 0)),
        onehot(src_col, iota((edge_rows, want_send.shape[1]), 1)),
    )
    want_send[...] = want.astype(jnp.bfloat16)
    want_copies = [
        remote(
            1, k, want_send.at[pl.ds(k * CAP, CAP)], want_recv.at[pl.ds(k * CAP, CAP)], ahead(k)
        )
        for k in range(PARTNERS)
    ]
    for k in ORDER:
        want_copies[k].start()
    sends += want_copies

    for c in range(CHUNKS):
        piece = pool_row[:, c * step_rows : (c + 1) * step_rows] - PARTNERS * cn
        own += dot(
            onehot(piece, iota((cn, step_rows), 0)), fine[pl.ds(c * step_rows, step_rows), :]
        )
    take_away = onehot(to_column(away_row), iota((edge_rows, PARTNERS * CAP), 1))
    take_own = onehot(to_column(own_src_row), iota((edge_rows, cn), 1))
    take_dst = onehot(to_column(dst_row), iota((edge_rows, cn), 1))
    add_dst = onehot(dst_row, iota((cn, edge_rows), 0))
    pool_col = to_column(pool_row)
    take_far[...] = onehot(pool_col, iota((fine_rows, PARTNERS * cn), 1))
    arrive(5 + CHUNKS, len(loads))
    edge_state = edges[...]

    for copy in pool_copies:
        copy.wait_recv()
    for k in range(PARTNERS):
        own += pool_recv[pl.ds(k * cn, cn), :].astype(jnp.float32)
    coarse = (own * 0.25).astype(jnp.bfloat16)
    for copy in want_copies:
        copy.wait_recv()

    for layer in range(LAYERS):
        rows_send[layer] = dot(want_recv[:, :cn], coarse).astype(jnp.bfloat16)
        row_copies = [
            remote(
                2 + layer,
                k,
                rows_send.at[layer, pl.ds(k * CAP, CAP)],
                rows_recv.at[layer, pl.ds(k * CAP, CAP)],
                behind(k),
            )
            for k in range(PARTNERS)
        ]
        for k in ORDER:
            row_copies[k].start()
        sends += row_copies
        mixed = dot(edge_state, ew1[layer, 2 * width :, :])
        mixed += dot(dot(take_own, coarse).astype(jnp.bfloat16), ew1[layer, :width, :])
        mixed += dot(dot(take_dst, coarse).astype(jnp.bfloat16), ew1[layer, width : 2 * width, :])
        node_mixed = dot(coarse, nw1[layer, :width, :])
        for copy in row_copies:
            copy.wait_recv()
        sender = dot(take_away, rows_recv[layer]).astype(jnp.bfloat16)
        mixed += dot(sender, ew1[layer, :width, :])
        hidden = jnp.maximum(mixed, 0.0).astype(jnp.bfloat16)
        update = layer_norm(dot(hidden, ew2[layer]))
        edge_state = (edge_state.astype(jnp.float32) + update).astype(jnp.bfloat16)
        summed = dot(add_dst, edge_state).astype(jnp.bfloat16)
        node_mixed += dot(summed, nw1[layer, width:, :])
        hidden = jnp.maximum(node_mixed, 0.0).astype(jnp.bfloat16)
        update = layer_norm(dot(hidden, nw2[layer]))
        coarse = (coarse.astype(jnp.float32) + update).astype(jnp.bfloat16)

    last_send[...] = coarse
    last_copies = [
        remote(2 + LAYERS, k, last_send, last_recv.at[pl.ds(k * cn, cn)], behind(k))
        for k in range(PARTNERS)
    ]
    for k in ORDER:
        last_copies[k].start()
    sends += last_copies
    take_base = onehot(pool_col - PARTNERS * cn, iota((fine_rows, cn), 1))
    lift_base[...] = fine[...].astype(jnp.float32) + dot(take_base, coarse)
    for copy in last_copies:
        copy.wait_recv()
    lift_rows[...] = last_recv[...]
    for copy in sends:
        copy.wait_send()


def lift_kernel(base, take, rows, out_hbm, out, store_sem):
    step_rows = base.shape[0] // CHUNKS
    stores = []
    for c in range(CHUNKS):
        part = pl.ds(c * step_rows, step_rows)
        out[part, :] = (base[part, :] + dot(take[part, :], rows[...])).astype(jnp.bfloat16)
        copy = pltpu.make_async_copy(out.at[part], out_hbm.at[part], store_sem.at[c])
        copy.start()
        stores.append(copy)
    for copy in stores:
        copy.wait()


def per_device(
    n,
    fine_latent,
    pool_owner,
    pool_local,
    edge_latent,
    src_owner,
    src_local,
    dst_local,
    edge_w1,
    edge_w2,
    node_w1,
    node_w2,
):
    fine_rows, width = fine_latent.shape
    edge_rows = edge_latent.shape[0]
    cn = fine_rows // FINE_PER_COARSE
    lanes = -(-cn // 128) * 128
    hbm = pl.BlockSpec(memory_space=pltpu.HBM)
    vmem = pl.BlockSpec(memory_space=pltpu.VMEM)
    bf16 = jnp.bfloat16
    stages = 3 + LAYERS
    base, take, rows = pl.pallas_call(
        functools.partial(kernel, n),
        out_shape=(
            pltpu.VMEM((fine_rows, width), jnp.float32),
            pltpu.VMEM((fine_rows, PARTNERS * cn), bf16),
            pltpu.VMEM((PARTNERS * cn, width), bf16),
        ),
        in_specs=[hbm] * 11,
        out_specs=(vmem, vmem, vmem),
        scratch_shapes=[
            pltpu.VMEM((1, fine_rows), jnp.int32),
            pltpu.VMEM((1, fine_rows), jnp.int32),
            pltpu.VMEM((1, edge_rows), jnp.int32),
            pltpu.VMEM((1, edge_rows), jnp.int32),
            pltpu.VMEM((1, edge_rows), jnp.int32),
            pltpu.VMEM((fine_rows, width), bf16),
            pltpu.VMEM((edge_rows, width), bf16),
            pltpu.VMEM(edge_w1.shape, bf16),
            pltpu.VMEM(edge_w2.shape, bf16),
            pltpu.VMEM(node_w1.shape, bf16),
            pltpu.VMEM(node_w2.shape, bf16),
            pltpu.VMEM((PARTNERS * cn, width), bf16),
            pltpu.VMEM((PARTNERS * cn, width), bf16),
            pltpu.VMEM((PARTNERS * CAP, lanes), bf16),
            pltpu.VMEM((PARTNERS * CAP, lanes), bf16),
            pltpu.VMEM((LAYERS, PARTNERS * CAP, width), bf16),
            pltpu.VMEM((LAYERS, PARTNERS * CAP, width), bf16),
            pltpu.VMEM((cn, width), bf16),
            pltpu.VMEM((PARTNERS * cn, width), bf16),
            pltpu.SemaphoreType.DMA((CHUNKS + 10,)),
            pltpu.SemaphoreType.DMA((stages, PARTNERS)),
            pltpu.SemaphoreType.DMA((stages, PARTNERS)),
        ],
        compiler_params=pltpu.CompilerParams(
            collective_id=0, has_side_effects=True, vmem_limit_bytes=60 * 1024 * 1024
        ),
    )(
        fine_latent,
        pool_owner.reshape(1, fine_rows),
        pool_local.reshape(1, fine_rows),
        edge_latent,
        src_owner.reshape(1, edge_rows),
        src_local.reshape(1, edge_rows),
        dst_local.reshape(1, edge_rows),
        edge_w1,
        edge_w2,
        node_w1,
        node_w2,
    )
    return pl.pallas_call(
        lift_kernel,
        out_shape=jax.ShapeDtypeStruct((fine_rows, width), bf16),
        in_specs=[vmem, vmem, vmem],
        out_specs=hbm,
        scratch_shapes=[
            pltpu.VMEM((fine_rows, width), bf16),
            pltpu.SemaphoreType.DMA((CHUNKS,)),
        ],
        compiler_params=pltpu.CompilerParams(vmem_limit_bytes=16 * 1024 * 1024),
    )(base, take, rows)


def solution(mesh):
    rows = P(("groups", "dom"), None)
    line = P(("groups", "dom"))
    return jax.shard_map(
        functools.partial(per_device, mesh.shape["dom"]),
        mesh=mesh,
        in_specs=(rows, rows, line, rows, rows, line, line, P(), P(), P(), P()),
        out_specs=rows,
        check_vma=False,
    )
```
